32 devices in a mesh: row: 4 (over x, core), col: 8 (over z, y).
Axes of the slice: x: 2, y: 2, z: 4, core: 2. Of those that a mesh axis runs over, the one named last changes fastest.
Arguments:
- activations: bfloat16 [256, 5120], P('col', 'row'), may hold values from -1.5 to 1.5
- grad_output: bfloat16 [256, 5120], P('col', 'row'), may hold values from -1.5 to 1.5
- gate_pre: bfloat16 [256, 25600], P('row', 'col'), may hold values from -6 to 6
- up_pre: bfloat16 [256, 25600], P('row', 'col'), may hold values from -6 to 6
- gate_weight: bfloat16 [5120, 25600], P('row', 'col'), may hold values from -0.078125 to 0.078125
- up_weight: bfloat16 [5120, 25600], P('row', 'col'), may hold values from -0.078125 to 0.078125
- down_weight: bfloat16 [25600, 5120], P('col', 'row'), may hold values from -0.0390625 to 0.0390625
Outputs:
- grad_input: float32 [256, 5120], P('col', 'row')
- grad_gate_weight: float32 [5120, 25600], P('row', 'col')
- grad_up_weight: float32 [5120, 25600], P('row', 'col')
- grad_down_weight: float32 [25600, 5120], P('col', 'row')
The draws below stay inside these ranges and needn't reach their ends.
All inputs are finite; a program needn't handle non-finite values.
Results may differ from the reference program's by a relative error of at most 0.0029.
Values may be sent and summed in bfloat16 or wider, within the bound.
A program may use at most 128 MiB of HBM per device.

```python
import jax
import jax.numpy as jnp

D = 5120
FF = 25600
TOKENS = 256


def strengthened(result, key, source, target, shards_of, factor):
    owner, partner = [(jnp.arange(result.shape[dim]) // (result.shape[dim] // shards_of)).reshape([-1 if axis == dim else 1 for axis in range(result.ndim)]) for dim in (source, target)]
    chosen = jax.random.permutation(key, shards_of)[partner]
    strong = (owner == chosen) | (owner == (partner + shards_of // 2) % shards_of)
    return jnp.where(strong, factor * result, result)


def block_scale(key, shape, split, smallest, high):
    factor_of, own = 1.0, jax.random.fold_in(key, 6)
    for axis_at, parts in split:
        heights = jnp.exp(jax.random.uniform(jax.random.fold_in(own, axis_at), (parts,), jnp.float32, smallest / len(split), high / len(split)))
        factor_of = factor_of * jnp.repeat(heights, shape[axis_at] // parts).reshape([-1 if axis == axis_at else 1 for axis in range(len(shape))])
    return factor_of


def scatter_about(rng, dims, deviation, bound, shards=(), held_as=jnp.bfloat16):
    result = deviation * jax.random.normal(rng, dims, jnp.float32)
    if shards:
        result = result * block_scale(rng, dims, shards, -0.22, 0.18)
    return jnp.clip(result, -bound, bound).astype(held_as)


def noise_with(stream_key, shape, deviation, bound, pieces, heavy, dtype=jnp.bfloat16):
    array = deviation * jax.random.normal(stream_key, shape, jnp.float32)
    if pieces:
        array = array * block_scale(stream_key, shape, pieces, -0.22, 0.18)
    return jnp.clip(strengthened(array, jax.random.fold_in(stream_key, 3), *heavy), -bound, bound).astype(dtype)


def setup_inputs(seed: int = 0) -> dict:
    key_list = jax.random.split(jax.random.key(seed), 8)
    activations = scatter_about(key_list[0], (TOKENS, D), 0.25, 1.5, ((0, 8), (1, 4)))
    grad_output = noise_with(key_list[1], (TOKENS, D), 0.25, 1.5, ((0, 8), (1, 4)), (1, 0, 8, 2.0))
    gate_pre = scatter_about(key_list[2], (TOKENS, FF), 1.0, 6.0, ((0, 4), (1, 8)))
    up_pre = scatter_about(key_list[3], (TOKENS, FF), 1.0, 6.0, ((0, 4), (1, 8)))
    gate_weight = scatter_about(key_list[4], (D, FF), D ** -0.5, 0.078125, ((0, 4), (1, 8)))
    up_weight = scatter_about(key_list[5], (D, FF), D ** -0.5, 0.078125, ((0, 4), (1, 8)))
    down_weight = scatter_about(key_list[6], (FF, D), FF ** -0.5, 0.0390625, ((0, 8), (1, 4)))
    return dict(activations=activations, grad_output=grad_output, gate_pre=gate_pre, up_pre=up_pre, gate_weight=gate_weight, up_weight=up_weight, down_weight=down_weight)


def swiglu_back(gate_vals, up_vals, grad_hidden):
    gate_wide = gate_vals.astype(jnp.float32)
    up_wide = up_vals.astype(jnp.float32)
    logistic = jax.nn.sigmoid(gate_wide)
    silu_val = gate_wide * logistic
    hidden = (silu_val * up_wide).astype(jnp.bfloat16)
    grad_gate = (grad_hidden * up_wide * logistic * (1.0 + gate_wide * (1.0 - logistic))).astype(jnp.bfloat16)
    grad_up = (grad_hidden * silu_val).astype(jnp.bfloat16)
    return hidden, grad_gate, grad_up


def reference(activations, grad_output, gate_pre, up_pre, gate_weight, up_weight, down_weight):
    grad_hidden = jnp.dot(grad_output, down_weight.T, preferred_element_type=jnp.float32)
    hidden, grad_gate, grad_up = swiglu_back(gate_pre, up_pre, grad_hidden)
    grad_down_weight = jnp.dot(hidden.T, grad_output, preferred_element_type=jnp.float32)
    grad_gate_weight = jnp.dot(activations.T, grad_gate, preferred_element_type=jnp.float32)
    grad_up_weight = jnp.dot(activations.T, grad_up, preferred_element_type=jnp.float32)
    grad_input = jnp.dot(grad_gate, gate_weight.T, preferred_element_type=jnp.float32) + jnp.dot(grad_up, up_weight.T, preferred_element_type=jnp.float32)
    return (grad_input, grad_gate_weight, grad_up_weight, grad_down_weight)
```

```python
import functools

import jax
import jax.numpy as jnp
from jax import lax
from jax.experimental import pallas as pl
from jax.experimental.pallas import tpu as pltpu
from jax.sharding import PartitionSpec as P

MESH = pl.DeviceIdType.MESH
VMEM = pl.BlockSpec(memory_space=pltpu.VMEM)


def right_trans(left, right):
    return lax.dot_general(
        left, right, (((1,), (1,)), ((), ())), preferred_element_type=jnp.float32
    )


class Gather:
    def __init__(self, buf, axis, size, block, send_sem, recv_sem, base):
        self.buf, self.axis, self.half, self.block = buf, axis, size // 2, block
        self.send_sem, self.recv_sem, self.base = send_sem, recv_sem, base
        self.me = lax.axis_index(axis)
        self.major, self.minor = self.me // 2, self.me % 2
        self.slots = size - 1

    def view(self, index, cols):
        start = pl.multiple_of(index * self.block, self.block)
        return self.buf.at[pl.ds(start, self.block), cols]

    def copy(self, index, target, slot, cols, at):
        sem = self.base + at * self.slots + slot
        return pltpu.make_async_remote_copy(
            src_ref=self.view(index, cols),
            dst_ref=self.view(index, cols),
            send_sem=self.send_sem.at[sem],
            recv_sem=self.recv_sem.at[sem],
            device_id={self.axis: target},
            device_id_type=MESH,
        )

    def pair(self):
        return self.major * 2 + 1 - self.minor

    def to_pair(self, cols, at):
        return self.copy(self.me, self.pair(), 0, cols, at)

    def to_peer(self, k, cols, at):
        target = lax.rem(self.major + k, self.half) * 2 + self.minor
        return self.copy(self.me, target, k, cols, at)

    def onward(self, k, cols, at):
        source = lax.rem(self.major - k + self.half, self.half) * 2 + self.minor
        return self.copy(source, self.pair(), self.half - 1 + k, cols, at)

    def start(self, cols=slice(None), at=0):
        for k in range(1, self.half):
            self.to_peer(k, cols, at).start()
        self.to_pair(cols, at).start()

    def forward(self, cols=slice(None), at=0):
        for k in range(1, self.half):
            self.to_peer(k, cols, at).wait_recv()
            self.onward(k, cols, at).start()

    def arrive(self, cols=slice(None), at=0):
        self.to_pair(cols, at).wait_recv()
        for k in range(1, self.half):
            self.onward(k, cols, at).wait_recv()

    def drain(self, cols=slice(None), at=0):
        self.to_pair(cols, at).wait_send()
        for k in range(1, self.half):
            self.to_peer(k, cols, at).wait_send()
            self.onward(k, cols, at).wait_send()


def middle_kernel(
    rows_n, cols_n, chunks,
    go_ref, act_ref, gate_ref, up_ref, down_hbm,
    go_all, act_all, hid_all, gg_all, gu_all,
    down, partial, sib, xsend, xrecv, own, send_sem, recv_sem, local_sem,
):
    half = rows_n // 2
    width_tokens = go_ref.shape[0]
    hidden_tokens, units = gate_ref.shape
    wide = units // chunks
    row = lax.axis_index("row")
    major, minor = row // 2, row % 2
    pair = major * 2 + 1 - minor

    load = pltpu.make_async_copy(down_hbm, down, local_sem)
    load.start()

    def cols(j):
        if chunks == 1:
            return slice(None)
        return pl.ds(pl.multiple_of(j * wide, wide), wide)

    base = 0
    go = Gather(go_all, "col", cols_n, width_tokens, send_sem, recv_sem, base)
    base += cols_n - 1
    act = Gather(act_all, "col", cols_n, width_tokens, send_sem, recv_sem, base)
    base += cols_n - 1
    hid = Gather(hid_all, "row", rows_n, hidden_tokens, send_sem, recv_sem, base)
    base += rows_n - 1
    gg = Gather(gg_all, "row", rows_n, hidden_tokens, send_sem, recv_sem, base)
    base += chunks * (rows_n - 1)
    gu = Gather(gu_all, "row", rows_n, hidden_tokens, send_sem, recv_sem, base)
    base += chunks * (rows_n - 1)
    sib_base = base
    base += chunks
    x_base = base

    barrier = pltpu.get_barrier_semaphore()
    for plan in (go, hid):
        pl.semaphore_signal(
            barrier, inc=1, device_id={plan.axis: plan.pair()}, device_id_type=MESH
        )
        for k in range(1, plan.half):
            target = lax.rem(plan.major + k, plan.half) * 2 + plan.minor
            pl.semaphore_signal(
                barrier, inc=1, device_id={plan.axis: target}, device_id_type=MESH
            )
    pl.semaphore_wait(barrier, cols_n // 2 + half)

    go_at = pl.ds(pl.multiple_of(go.me * width_tokens, width_tokens), width_tokens)
    go_all[go_at, :] = go_ref[...]
    go.start()

    row_at = pl.ds(pl.multiple_of(row * hidden_tokens, hidden_tokens), hidden_tokens)

    def hidden_step(j, carry):
        gate = gate_ref[:, cols(j)].astype(jnp.float32)
        up = up_ref[:, cols(j)].astype(jnp.float32)
        silu = gate * jax.nn.sigmoid(gate)
        hid_all[row_at, cols(j)] = (silu * up).astype(jnp.bfloat16)
        return carry

    lax.fori_loop(0, chunks, hidden_step, 0)
    hid.start()

    go.forward()
    act_all[go_at, :] = act_ref[...]
    act.start()
    load.wait()
    go.arrive()

    def sib_copy(j):
        return pltpu.make_async_remote_copy(
            src_ref=partial.at[:, 1 - minor, :, cols(j)],
            dst_ref=sib.at[:, :, cols(j)],
            send_sem=send_sem.at[sib_base + j],
            recv_sem=recv_sem.at[sib_base + j],
            device_id={"row": pair},
            device_id_type=MESH,
        )

    def x_copy(k, j):
        target = lax.rem(major + k, half) * 2 + minor
        sem = x_base + j * (half - 1) + k - 1
        return pltpu.make_async_remote_copy(
            src_ref=xsend.at[k - 1, :, cols(j)],
            dst_ref=xrecv.at[k - 1, :, cols(j)],
            send_sem=send_sem.at[sem],
            recv_sem=recv_sem.at[sem],
            device_id={"row": target},
            device_id_type=MESH,
        )

    def product_step(j, carry):
        if chunks == 1:
            weight = down[...]
        else:
            weight = down[pl.ds(pl.multiple_of(j * wide, wide), wide), :]
        total = right_trans(go_all[...], weight)
        partial[:, :, :, cols(j)] = total.reshape(half, 2, hidden_tokens, wide)
        sib_copy(j).start()
        return carry

    lax.fori_loop(0, chunks, product_step, 0)

    def pair_step(j, carry):
        sib_copy(j).wait_recv()
        for k in range(1, half):
            block = lax.rem(major + k, half)
            total = partial[block, minor, :, cols(j)] + sib[block, :, cols(j)]
            xsend[k - 1, :, cols(j)] = total.astype(jnp.bfloat16)
            x_copy(k, j).start()
        own[:, cols(j)] = partial[major, minor, :, cols(j)] + sib[major, :, cols(j)]
        return carry

    lax.fori_loop(0, chunks, pair_step, 0)

    hid.forward()
    act.forward()

    def grad_step(j, carry):
        grad = own[:, cols(j)]
        for k in range(1, half):
            x_copy(k, j).wait_recv()
            grad = grad + xrecv[k - 1, :, cols(j)].astype(jnp.float32)
        gate = gate_ref[:, cols(j)].astype(jnp.float32)
        up = up_ref[:, cols(j)].astype(jnp.float32)
        logistic = jax.nn.sigmoid(gate)
        gg_all[row_at, cols(j)] = (
            grad * up * logistic * (1.0 + gate * (1.0 - logistic))
        ).astype(jnp.bfloat16)
        gg.start(cols(j), j)
        gu_all[row_at, cols(j)] = (grad * (gate * logistic)).astype(jnp.bfloat16)
        gu.start(cols(j), j)
        return carry

    lax.fori_loop(0, chunks, grad_step, 0)

    def pass_step(j, carry):
        gg.forward(cols(j), j)
        gu.forward(cols(j), j)
        return carry

    lax.fori_loop(0, chunks, pass_step, 0)

    act.arrive()
    hid.arrive()
    go.drain()
    act.drain()
    hid.drain()

    def end_step(j, carry):
        for plan in (gg, gu):
            plan.arrive(cols(j), j)
            plan.drain(cols(j), j)
        sib_copy(j).wait_send()
        for k in range(1, half):
            x_copy(k, j).wait_send()
        return carry

    lax.fori_loop(0, chunks, end_step, 0)


def middle(rows_n, cols_n, grad_output, activations, gate_pre, up_pre, down_weight):
    width_tokens, features = grad_output.shape
    hidden_tokens, units = gate_pre.shape
    tokens = width_tokens * cols_n
    chunks = 5 if units % 640 == 0 else 1
    half = rows_n // 2
    sems = 2 * (cols_n - 1) + (1 + 2 * chunks) * (rows_n - 1) + chunks * half
    narrow = jax.ShapeDtypeStruct((tokens, features), jnp.bfloat16)
    broad = jax.ShapeDtypeStruct((tokens, units), jnp.bfloat16)
    peers = max(half - 1, 1)
    return pl.pallas_call(
        functools.partial(middle_kernel, rows_n, cols_n, chunks),
        out_shape=(narrow, narrow, broad, broad, broad),
        in_specs=[VMEM] * 4 + [pl.BlockSpec(memory_space=pl.ANY)],
        out_specs=(VMEM,) * 5,
        scratch_shapes=[
            pltpu.VMEM((units, features), jnp.bfloat16),
            pltpu.VMEM((half, 2, hidden_tokens, units), jnp.float32),
            pltpu.VMEM((half, hidden_tokens, units), jnp.float32),
            pltpu.VMEM((peers, hidden_tokens, units), jnp.bfloat16),
            pltpu.VMEM((peers, hidden_tokens, units), jnp.bfloat16),
            pltpu.VMEM((hidden_tokens, units), jnp.float32),
            pltpu.SemaphoreType.DMA((sems,)),
            pltpu.SemaphoreType.DMA((sems,)),
            pltpu.SemaphoreType.DMA,
        ],
        compiler_params=pltpu.CompilerParams(
            collective_id=0, has_side_effects=True, vmem_limit_bytes=48 * 1024 * 1024
        ),
        cost_estimate=pl.CostEstimate(
            flops=2 * tokens * features * units,
            bytes_accessed=2 * units * features,
            transcendentals=0,
        ),
    )(grad_output, activations, gate_pre, up_pre, down_weight)


def outer_kernel(left_ref, right_ref, out_ref):
    out_ref[...] = lax.dot_general(
        left_ref[...],
        right_ref[...],
        (((0,), (0,)), ((), ())),
        preferred_element_type=jnp.float32,
    )


def left_trans(left, right):
    tokens, height = left.shape
    width = right.shape[1]
    tile = height
    for steps in (10, 5, 4, 2):
        if height % (128 * steps) == 0 and (height // steps) * width >= 2**19:
            tile = height // steps
            break
    return pl.pallas_call(
        outer_kernel,
        grid=(height // tile,),
        out_shape=jax.ShapeDtypeStruct((height, width), jnp.float32),
        in_specs=[
            pl.BlockSpec((tokens, tile), lambda i: (0, i)),
            pl.BlockSpec((tokens, width), lambda i: (0, 0)),
        ],
        out_specs=pl.BlockSpec((tile, width), lambda i: (i, 0)),
        compiler_params=pltpu.CompilerParams(vmem_limit_bytes=40 * 1024 * 1024),
        cost_estimate=pl.CostEstimate(
            flops=2 * tokens * height * width,
            bytes_accessed=4 * height * width + 2 * tokens * (height + width),
            transcendentals=0,
        ),
    )(left, right)


def shards(
    rows_n, cols_n,
    activations, grad_output, gate_pre, up_pre, gate_weight, up_weight, down_weight,
):
    grad_rows, act_rows, hidden, grad_gate, grad_up = middle(
        rows_n, cols_n, grad_output, activations, gate_pre, up_pre, down_weight
    )
    share = right_trans(grad_gate, gate_weight) + right_trans(grad_up, up_weight)
    share, grad_rows, act_rows, hidden, grad_gate, grad_up = lax.optimization_barrier(
        (share, grad_rows, act_rows, hidden, grad_gate, grad_up)
    )
    grad_input = lax.psum_scatter(share, "col", scatter_dimension=0, tiled=True)
    grad_gate_weight = left_trans(act_rows, grad_gate)
    grad_up_weight = left_trans(act_rows, grad_up)
    grad_down_weight = left_trans(hidden, grad_rows)
    return (grad_input, grad_gate_weight, grad_up_weight, grad_down_weight)


def solution(mesh):
    placed = (
        P("col", "row"),
        P("col", "row"),
        P("row", "col"),
        P("row", "col"),
        P("row", "col"),
        P("row", "col"),
        P("col", "row"),
    )
    return jax.shard_map(
        functools.partial(shards, mesh.shape["row"], mesh.shape["col"]),
        mesh=mesh,
        in_specs=placed,
        out_specs=(P("col", "row"), P("row", "col"), P("row", "col"), P("col", "row")),
        check_vma=False,
    )
```
